32 devices in a mesh: ctx: 8 (over y, x, core), fsdp: 4 (over z).
Axes of the slice: x: 2, y: 2, z: 4, core: 2. Of those that a mesh axis runs over, the one named last changes fastest.
Arguments:
- layer_input: bfloat16 [4, 1024, 768], P('fsdp', 'ctx'), may hold values from -6 to 6
- cotangent: bfloat16 [4, 1024, 768], P('fsdp', 'ctx'), may hold values from -6 to 6
- block_order: int32 [16], replicated, may hold values from 0 to 15, each once
- boundary: int32 [4], P('fsdp'), may hold values from 961 to 1023
- attn_gain: float32 [768], replicated, may hold values from 0.5 to 1.5
- attn_shift: float32 [768], replicated, may hold values from -1.5 to 1.5
- mlp_gain: float32 [768], replicated, may hold values from 0.5 to 1.5
- mlp_shift: float32 [768], replicated, may hold values from -1.5 to 1.5
- joined_weight: bfloat16 [768, 2304], P('fsdp'), may hold values from -0.3125 to 0.3125
- joined_bias: float32 [2304], replicated, may hold values from -1.5 to 1.5
- attn_weight: bfloat16 [768, 768], P(None, 'fsdp'), may hold values from -0.875 to 0.875
- attn_bias: float32 [768], replicated, may hold values from -1.5 to 1.5
- up_weight: bfloat16 [768, 3072], P('fsdp'), may hold values from -0.21875 to 0.21875
- up_bias: float32 [3072], replicated, may hold values from -1.5 to 1.5
- down_weight: bfloat16 [3072, 768], P(None, 'fsdp'), may hold values from -0.109375 to 0.109375
- down_bias: float32 [768], replicated, may hold values from -1.5 to 1.5
Outputs:
- layer_output: bfloat16 [4, 1024, 768], P('fsdp', 'ctx')
- input_grad: float32 [4, 1024, 768], P('fsdp', 'ctx')
- dattn_gain: float32 [768], replicated
- dattn_shift: float32 [768], replicated
- dmlp_gain: float32 [768], replicated
- dmlp_shift: float32 [768], replicated
- dfused_weight: float32 [768, 2304], P('fsdp')
- dfused_bias: float32 [2304], replicated
- dattn_weight: float32 [768, 768], P(None, 'fsdp')
- dattn_bias: float32 [768], replicated
- dup_weight: float32 [768, 3072], P('fsdp')
- dup_bias: float32 [3072], replicated
- ddown_weight: float32 [3072, 768], P(None, 'fsdp')
- ddown_bias: float32 [768], replicated
The draws below stay inside these ranges and needn't reach their ends.
All inputs are finite; a program needn't handle non-finite values.
Results may differ from the reference program's by a relative error of at most 0.014.
The reference program's roundings to bfloat16 on the way count: a program that leaves them out, or rounds other values in their place, can miss the bound.
Values may be sent and summed in bfloat16 or wider, within the bound.
A program may use at most 192 MiB of HBM per device.

```python
import jax
import jax.numpy as jnp
from jax import lax

D = 768
HEADS = 12
HEAD = 64
ROT = 16
FF = 3072
TOK_DEV = 128
SEQ_LEN = 1024
SEQS = 4
HALF = 64
N_CTX = 8


def set_ends(entries, own_key, low, top_value):
    place = [jax.random.randint(jax.random.fold_in(own_key, axis), (), 0, length) for axis, length in enumerate(entries.shape)]
    longest = entries.shape.index(max(entries.shape))
    beside = place[:longest] + [(place[longest] + 1) % entries.shape[longest]] + place[longest + 1:]
    return entries.at[tuple(place)].set(low).at[tuple(beside)].set(top_value)


def block_levels(own_key, shape, cuts, least, largest):
    def one(axis_at, shards_of):
        draws = jax.random.uniform(jax.random.fold_in(jax.random.fold_in(own_key, 6), axis_at), (shards_of,), jnp.float32, least / len(cuts), largest / len(cuts))
        return jnp.repeat(jnp.exp(draws), shape[axis_at] // shards_of).reshape((-1,) + (1,) * (len(shape) - axis_at - 1))

    factor_of = one(*cuts[0])
    for cut in cuts[1:]:
        factor_of = factor_of * one(*cut)
    return factor_of


def normal_values(stream_key, dims, scale, bound, shards=(), held_as=jnp.bfloat16):
    entries = scale * jax.random.normal(stream_key, dims, jnp.float32)
    if shards:
        entries = entries * block_levels(stream_key, dims, shards, -0.22, 0.18)
    return jnp.clip(entries, -bound, bound).astype(held_as)


def setup_inputs(seed: int = 0) -> dict:
    key_of = jax.random.split(jax.random.key(seed), 17)
    layer_input = normal_values(key_of[0], (SEQS, SEQ_LEN, D), 1.0, 6.0, ((0, 4), (1, 8)))
    cotangent = normal_values(key_of[1], (SEQS, SEQ_LEN, D), 1.0, 6.0, ((0, 4), (1, 8)))
    block_order = jax.random.permutation(key_of[2], 2 * N_CTX).astype(jnp.int32)
    boundary = set_ends(jax.random.randint(key_of[3], (SEQS,), SEQ_LEN - TOK_DEV // 2 + 1, SEQ_LEN), jax.random.fold_in(key_of[3], 1), SEQ_LEN - TOK_DEV // 2 + 1, SEQ_LEN - 1).astype(jnp.int32)
    attn_gain = jnp.clip(1.0 + 0.1 * jax.random.normal(key_of[4], (D,), jnp.float32), 0.5, 1.5)
    attn_shift = normal_values(key_of[5], (D,), 0.3, 1.5, (), jnp.float32)
    mlp_gain = jnp.clip(1.0 + 0.1 * jax.random.normal(key_of[6], (D,), jnp.float32), 0.5, 1.5)
    mlp_shift = normal_values(key_of[7], (D,), 0.3, 1.5, (), jnp.float32)
    joined_weight = normal_values(key_of[8], (D, 3 * D), (D // 2) ** -0.5, 0.3125, ((0, 4),))
    joined_bias = normal_values(key_of[9], (3 * D,), 0.3, 1.5, (), jnp.float32)
    attn_weight = normal_values(key_of[10], (D, D), (max(1, D * 64 // SEQ_LEN)) ** -0.5, 0.875, ((1, 4),))
    attn_bias = normal_values(key_of[11], (D,), 0.3, 1.5, (), jnp.float32)
    up_weight = normal_values(key_of[12], (D, FF), D ** -0.5, 0.21875, ((0, 4),))
    up_bias = normal_values(key_of[13], (FF,), 0.3, 1.5, (), jnp.float32)
    down_weight = normal_values(key_of[14], (FF, D), FF ** -0.5, 0.109375, ((1, 4),))
    down_bias = normal_values(key_of[15], (D,), 0.3, 1.5, (), jnp.float32)
    return {"layer_input": layer_input, "cotangent": cotangent, "block_order": block_order, "boundary": boundary, "attn_gain": attn_gain, "attn_shift": attn_shift, "mlp_gain": mlp_gain, "mlp_shift": mlp_shift, "joined_weight": joined_weight, "joined_bias": joined_bias, "attn_weight": attn_weight, "attn_bias": attn_bias, "up_weight": up_weight, "up_bias": up_bias, "down_weight": down_weight, "down_bias": down_bias}


@jax.custom_vjp
def low(v):
    return lax.optimization_barrier(v.astype(jnp.bfloat16)).astype(jnp.float32)

@jax.custom_vjp
def low_back(v):
    return v

def low_keep(v):
    return (low(v), None)

def low_pass(kept, grad):
    return (grad,)

def back_keep(v):
    return (v, None)

def back_low(kept, grad):
    return (low(grad),)
low.defvjp(low_keep, low_pass)
low_back.defvjp(back_keep, back_low)
epsilon = 1e-05
highest = lax.Precision.HIGHEST

def matmul(left, right):
    return jnp.dot(left, right, precision=highest)

def normalize(value, gain, shift):
    average = lax.optimization_barrier(jnp.mean(value, -1, keepdims=True))
    centered = value - average
    spread = lax.optimization_barrier(jnp.mean(centered * centered, -1, keepdims=True))
    return centered * lax.rsqrt(spread + epsilon) * gain + shift

def rotary(tensor, places):
    half = ROT // 2
    freq = 10000.0 ** (-2.0 * jnp.arange(half, dtype=jnp.float32) / ROT)
    angles = places.astype(jnp.float32)[:, None] * freq[None, :]
    cosine = jnp.cos(angles)[:, None, :]
    sine = jnp.sin(angles)[:, None, :]
    first = tensor[..., :half]
    second = tensor[..., half:ROT]
    return jnp.concatenate([first * cosine - second * sine, second * cosine + first * sine, tensor[..., ROT:]], -1)

def forward(hidden, attn_gain, attn_shift, mlp_gain, mlp_shift, joined_weight, joined_bias, attn_weight, attn_bias, up_weight, up_bias, down_weight, down_bias, places, documents):
    length = hidden.shape[0]
    norm_attn = low(normalize(hidden, attn_gain, attn_shift))
    norm_mlp = low(normalize(hidden, mlp_gain, mlp_shift))
    joined = low_back(matmul(norm_attn, joined_weight)) + joined_bias
    query = low(rotary(joined[:, :D].reshape(length, HEADS, HEAD), places))
    key = low(rotary(joined[:, D:2 * D].reshape(length, HEADS, HEAD), places))
    value = low(joined[:, 2 * D:].reshape(length, HEADS, HEAD))
    block_rows = min(512, length)
    scale = HEAD ** (-0.5)

    @jax.checkpoint
    def attend(index):
        begin = index * block_rows
        block = lax.dynamic_slice_in_dim(query, begin, block_rows, 0)
        block_places = lax.dynamic_slice_in_dim(places, begin, block_rows, 0)
        block_docs = lax.dynamic_slice_in_dim(documents, begin, block_rows, 0)
        valid = (places[None, :] <= block_places[:, None]) & (documents[None, :] == block_docs[:, None])
        scores = low_back(jnp.einsum('qhd,khd->hqk', block, key, precision=highest) * scale)
        scores = jnp.where(valid[None], scores, -1e+30)
        top = lax.optimization_barrier(jnp.max(scores, -1, keepdims=True))
        logsum = top + jnp.log(lax.optimization_barrier(jnp.sum(jnp.exp(scores - top), -1, keepdims=True)))
        prob = low(jnp.where(valid[None], jnp.exp(scores - logsum), 0.0))
        return jnp.einsum('hqk,khd->qhd', prob, value, precision=highest)
    mixed = lax.map(attend, jnp.arange(length // block_rows, dtype=jnp.int32))
    mix = low_back(low(mixed.reshape(length, D)))
    attn = matmul(mix, attn_weight) + attn_bias
    upper = low_back(matmul(norm_mlp, up_weight)) + up_bias
    act = low(jax.nn.gelu(upper, approximate=False))
    return hidden + attn + matmul(act, down_weight) + down_bias

def reference(layer_input, cotangent, block_order, boundary, attn_gain, attn_shift, mlp_gain, mlp_shift, joined_weight, joined_bias, attn_weight, attn_bias, up_weight, up_bias, down_weight, down_bias):
    storage = jnp.arange(SEQ_LEN, dtype=jnp.int32)
    places = (block_order[storage // HALF] * HALF + storage % HALF).astype(jnp.int32)
    params = tuple((p.astype(jnp.float32) for p in (attn_gain, attn_shift, mlp_gain, mlp_shift, joined_weight, joined_bias, attn_weight, attn_bias, up_weight, up_bias, down_weight, down_bias)))

    def sequence_step(carry, item):
        hidden, tangent, cutoff = item
        documents = (places >= cutoff).astype(jnp.int32)

        def local(*values):
            return forward(*values, places, documents)
        result, pull = jax.vjp(local, hidden.astype(jnp.float32), *params)
        grads = pull(tangent.astype(jnp.float32))
        carry = tuple((c + g for c, g in zip(carry, grads[1:])))
        return (carry, (result.astype(jnp.bfloat16), grads[0]))
    zeros = tuple((jnp.zeros_like(p) for p in params))
    sums, (outputs, input_grads) = lax.scan(sequence_step, zeros, (layer_input, cotangent, boundary))
    return (outputs, input_grads, sums[0], sums[1], sums[2], sums[3], sums[4], sums[5], sums[6], sums[7], sums[8], sums[9], sums[10], sums[11])
```

```python
import jax
import jax.numpy as jnp
from jax import lax
from jax.experimental import pallas as pl
from jax.experimental.pallas import tpu as pltpu
from jax.sharding import PartitionSpec as P

HEADS = 12
HEAD = 64
ROT = 16


epsilon = 1e-05
masked_score = -1e30
contract_rows = (((0,), (0,)), ((), ()))
contract_cols = (((1,), (1,)), ((), ()))


def place_lookup(block_order, begin, count, half):
    storage = begin + jnp.arange(count, dtype=jnp.int32)
    slots = storage // half
    table = jnp.arange(block_order.shape[0], dtype=jnp.int32)
    chosen = jnp.sum(jnp.where(slots[:, None] == table[None, :], block_order[None, :], 0), axis=1)
    return chosen * half + storage % half


def normalize_parts(value):
    average = jnp.mean(value, -1, keepdims=True)
    centered = value - average
    inverse = lax.rsqrt(jnp.mean(centered * centered, -1, keepdims=True) + epsilon)
    return (centered * inverse, inverse)


def norm_back(d_norm, normal, inverse, gain):
    scaled = d_norm * gain
    inner = (
        scaled
        - jnp.mean(scaled, -1, keepdims=True)
        - normal * jnp.mean(scaled * normal, -1, keepdims=True)
    )
    return (inner * inverse, jnp.sum(d_norm * normal, 0), jnp.sum(d_norm, 0))


def rotary_tables(places):
    half = ROT // 2
    freq = 10000.0 ** (-2.0 * jnp.arange(half, dtype=jnp.float32) / ROT)
    angles = places.astype(jnp.float32)[:, None] * freq[None, :]
    return (jnp.cos(angles)[:, None, :], jnp.sin(angles)[:, None, :])


def rotate(tensor, cosine, sine):
    half = ROT // 2
    first = tensor[..., :half]
    second = tensor[..., half:ROT]
    return jnp.concatenate(
        [first * cosine - second * sine, second * cosine + first * sine, tensor[..., ROT:]], -1
    )


def rotate_back(tensor, cosine, sine):
    half = ROT // 2
    first = tensor[..., :half]
    second = tensor[..., half:ROT]
    return jnp.concatenate(
        [first * cosine + second * sine, second * cosine - first * sine, tensor[..., ROT:]], -1
    )


def pair_terms(
    query_heads,
    query_pl,
    query_dc,
    mix_grad,
    log_total,
    delta_rows,
    key_heads,
    value_heads,
    key_pl,
    key_dc,
    scale,
):
    scores = (
        jnp.einsum("qhd,khd->hqk", query_heads, key_heads, preferred_element_type=jnp.float32)
        * scale
    )
    valid = ((key_pl[None, :] <= query_pl[:, None]) & (key_dc[None, :] == query_dc[:, None]))[None]
    scores = jnp.where(valid, scores, masked_score)
    prob = jnp.where(valid, jnp.exp(scores - log_total[..., None]), 0.0)
    d_prob = jnp.einsum("qhd,khd->hqk", mix_grad, value_heads, preferred_element_type=jnp.float32)
    d_score = (prob * (d_prob - delta_rows[..., None])).astype(jnp.bfloat16)
    return (prob, d_score)


def local(
    layer_input,
    cotangent,
    block_order,
    boundary,
    attn_gain,
    attn_shift,
    mlp_gain,
    mlp_shift,
    joined_weight,
    joined_bias,
    attn_weight,
    attn_bias,
    up_weight,
    up_bias,
    down_weight,
    down_bias,
):
    local_rows = layer_input.shape[1]
    width = layer_input.shape[2]
    context = lax.axis_size("ctx")
    length = local_rows * context
    half = local_rows // 2
    blocks = 2 * context
    key_tile = min(512, length)
    tiles_all = length // key_tile
    scale = HEAD ** (-0.5)
    cutoff = boundary[0]
    hidden = layer_input[0].astype(jnp.float32)
    grad_out = cotangent[0]
    my_index = lax.axis_index("ctx")
    begin = my_index * local_rows
    query_places = place_lookup(block_order, begin, local_rows, half)
    query_docs = (query_places >= cutoff).astype(jnp.int32)
    cosine, sine = rotary_tables(query_places)
    table = jnp.arange(blocks, dtype=jnp.int32)
    inverse_order = jnp.sum(
        jnp.where(block_order[None, :] == table[:, None], table[None, :], 0), axis=1
    )

    def place_order(whole):
        columns = whole.shape[1]
        return jnp.take(whole.reshape(blocks, half, columns), inverse_order, axis=0).reshape(
            length, columns
        )

    def block_first(index):
        return lax.dynamic_index_in_dim(block_order, 2 * my_index + index, 0, keepdims=False) * half

    normal, inverse = normalize_parts(hidden)
    norm_attn = (normal * attn_gain + attn_shift).astype(jnp.bfloat16)
    norm_mlp = (normal * mlp_gain + mlp_shift).astype(jnp.bfloat16)
    joined_full, up_full = (
        lax.all_gather(joined_weight, "fsdp", axis=0, tiled=True),
        lax.all_gather(up_weight, "fsdp", axis=0, tiled=True),
    )
    attn_full, down_full = (
        lax.all_gather(attn_weight, "fsdp", axis=1, tiled=True),
        lax.all_gather(down_weight, "fsdp", axis=1, tiled=True),
    )
    joined_lin = jnp.dot(norm_attn, joined_full, preferred_element_type=jnp.float32)
    up_lin = jnp.dot(norm_mlp, up_full, preferred_element_type=jnp.float32)
    joined = joined_lin + joined_bias
    queries = (
        rotate(joined[:, :width].reshape(local_rows, HEADS, HEAD), cosine, sine)
        .astype(jnp.bfloat16)
        .reshape(local_rows, width)
    )
    keys = (
        rotate(joined[:, width : 2 * width].reshape(local_rows, HEADS, HEAD), cosine, sine)
        .astype(jnp.bfloat16)
        .reshape(local_rows, width)
    )
    values = joined[:, 2 * width :].astype(jnp.bfloat16)
    kv_whole = lax.all_gather(jnp.concatenate([keys, values], 1), "ctx", axis=0, tiled=True)
    kv_ordered = place_order(kv_whole)

    def key_block_at(index):
        start = index * key_tile
        block = lax.dynamic_slice_in_dim(kv_ordered, start, key_tile, 0)
        key_pl = start + jnp.arange(key_tile, dtype=jnp.int32)
        key_dc = (key_pl >= cutoff).astype(jnp.int32)
        return (
            block[:, :width].reshape(key_tile, HEADS, HEAD),
            block[:, width:].reshape(key_tile, HEADS, HEAD),
            key_pl,
            key_dc,
        )

    mixtures = []
    tops = []
    totals = []
    for part in range(2):
        q_heads = queries[part * half : (part + 1) * half].reshape(half, HEADS, HEAD)
        q_pl = query_places[part * half : (part + 1) * half]
        q_dc = query_docs[part * half : (part + 1) * half]
        reach = (block_first(part) + half + key_tile - 1) // key_tile

        def forward_step(index, state, q_heads=q_heads, q_pl=q_pl, q_dc=q_dc):
            mixture, top, total = state
            key_heads, value_heads, key_pl, key_dc = key_block_at(index)
            scores = (
                jnp.einsum("qhd,khd->hqk", q_heads, key_heads, preferred_element_type=jnp.float32)
                * scale
            )
            valid = ((key_pl[None, :] <= q_pl[:, None]) & (key_dc[None, :] == q_dc[:, None]))[None]
            scores = jnp.where(valid, scores, masked_score)
            new_top = jnp.maximum(top, jnp.max(scores, -1))
            weights = jnp.where(valid, jnp.exp(scores - new_top[..., None]), 0.0)
            factor = jnp.exp(top - new_top)
            total = total * factor + jnp.sum(weights, -1)
            mixture = mixture * factor.T[:, :, None] + jnp.einsum(
                "hqk,khd->qhd",
                weights.astype(jnp.bfloat16),
                value_heads,
                preferred_element_type=jnp.float32,
            )
            return (mixture, new_top, total)

        start_state = (
            jnp.zeros((half, HEADS, HEAD), jnp.float32),
            jnp.full((HEADS, half), masked_score, jnp.float32),
            jnp.zeros((HEADS, half), jnp.float32),
        )
        mixture, top, total = lax.fori_loop(jnp.int32(0), reach, forward_step, start_state)
        mixtures.append(mixture)
        tops.append(top)
        totals.append(total)
    mixture = jnp.concatenate(mixtures, 0)
    top = jnp.concatenate(tops, 1)
    total = jnp.concatenate(totals, 1)
    logsum = top + jnp.log(total)
    mixed = mixture / total.T[:, :, None]
    mix_low = mixed.reshape(local_rows, width).astype(jnp.bfloat16)
    upper = up_lin + up_bias
    act, gelu_pull = jax.vjp(lambda argument: jax.nn.gelu(argument, approximate=False), upper)
    act_low = act.astype(jnp.bfloat16)
    branches = jnp.dot(mix_low, attn_full, preferred_element_type=jnp.float32) + jnp.dot(
        act_low, down_full, preferred_element_type=jnp.float32
    )
    layer_output = (hidden + branches + attn_bias + down_bias).astype(jnp.bfloat16)
    d_attn = lax.dot_general(grad_out, attn_full, contract_cols, preferred_element_type=jnp.float32)
    d_act = lax.dot_general(grad_out, down_full, contract_cols, preferred_element_type=jnp.float32)
    d_mix_flat = d_attn.astype(jnp.bfloat16)
    d_mix = d_mix_flat.reshape(local_rows, HEADS, HEAD)
    delta = jnp.einsum("qhd,qhd->hq", d_mix.astype(jnp.float32), mixed)
    d_up = gelu_pull(d_act)[0]
    d_up_low = d_up.astype(jnp.bfloat16)
    query_grads = []
    for part in range(2):
        q_heads = queries[part * half : (part + 1) * half].reshape(half, HEADS, HEAD)
        q_pl = query_places[part * half : (part + 1) * half]
        q_dc = query_docs[part * half : (part + 1) * half]
        g_heads = d_mix[part * half : (part + 1) * half]
        log_rows = logsum[:, part * half : (part + 1) * half]
        delta_part = delta[:, part * half : (part + 1) * half]
        reach = (block_first(part) + half + key_tile - 1) // key_tile

        def query_step(
            index,
            d_query,
            q_heads=q_heads,
            q_pl=q_pl,
            q_dc=q_dc,
            g_heads=g_heads,
            log_rows=log_rows,
            delta_part=delta_part,
        ):
            key_heads, value_heads, key_pl, key_dc = key_block_at(index)
            prob, d_score = pair_terms(
                q_heads,
                q_pl,
                q_dc,
                g_heads,
                log_rows,
                delta_part,
                key_heads,
                value_heads,
                key_pl,
                key_dc,
                scale,
            )
            return (
                d_query
                + jnp.einsum("hqk,khd->qhd", d_score, key_heads, preferred_element_type=jnp.float32)
                * scale
            )

        query_grads.append(
            lax.fori_loop(
                jnp.int32(0), reach, query_step, jnp.zeros((half, HEADS, HEAD), jnp.float32)
            )
        )
    d_query = jnp.concatenate(query_grads, 0)
    packed_whole = lax.all_gather(
        jnp.concatenate([queries, d_mix_flat], 1), "ctx", axis=0, tiled=True
    )
    stats_whole = lax.all_gather(jnp.concatenate([logsum.T, delta.T], 1), "ctx", axis=0, tiled=True)
    packed_ordered = place_order(packed_whole)
    stats_ordered = place_order(stats_whole)
    key_grads = []
    value_grads = []
    for part in range(2):
        own_keys = keys[part * half : (part + 1) * half].reshape(half, HEADS, HEAD)
        own_values = values[part * half : (part + 1) * half].reshape(half, HEADS, HEAD)
        own_pl = query_places[part * half : (part + 1) * half]
        own_dc = query_docs[part * half : (part + 1) * half]
        first_tile = block_first(part) // key_tile

        def owner_step(
            index, state, own_keys=own_keys, own_values=own_values, own_pl=own_pl, own_dc=own_dc
        ):
            start = index * key_tile
            block = lax.dynamic_slice_in_dim(packed_ordered, start, key_tile, 0)
            stat_block = lax.dynamic_slice_in_dim(stats_ordered, start, key_tile, 0)
            q_heads = block[:, :width].reshape(key_tile, HEADS, HEAD)
            g_heads = block[:, width:].reshape(key_tile, HEADS, HEAD)
            q_pl = start + jnp.arange(key_tile, dtype=jnp.int32)
            q_dc = (q_pl >= cutoff).astype(jnp.int32)
            prob, d_score = pair_terms(
                q_heads,
                q_pl,
                q_dc,
                g_heads,
                stat_block[:, :HEADS].T,
                stat_block[:, HEADS:].T,
                own_keys,
                own_values,
                own_pl,
                own_dc,
                scale,
            )
            d_key = (
                jnp.einsum("hqk,qhd->khd", d_score, q_heads, preferred_element_type=jnp.float32)
                * scale
            )
            d_value = jnp.einsum(
                "hqk,qhd->khd",
                prob.astype(jnp.bfloat16),
                g_heads,
                preferred_element_type=jnp.float32,
            )
            return (state[0] + d_key, state[1] + d_value)

        zero_heads = jnp.zeros((half, HEADS, HEAD), jnp.float32)
        part_key, part_value = lax.fori_loop(
            first_tile, jnp.int32(tiles_all), owner_step, (zero_heads, zero_heads)
        )
        key_grads.append(part_key)
        value_grads.append(part_value)
    key_grad_heads = jnp.concatenate(key_grads, 0)
    value_grad_rows = jnp.concatenate(value_grads, 0).reshape(local_rows, width)
    d_joined = jnp.concatenate(
        [
            rotate_back(d_query, cosine, sine).reshape(local_rows, width),
            rotate_back(key_grad_heads, cosine, sine).reshape(local_rows, width),
            value_grad_rows,
        ],
        1,
    )
    d_joined_low = d_joined.astype(jnp.bfloat16)
    d_norm_attn = lax.dot_general(
        d_joined_low, joined_full, contract_cols, preferred_element_type=jnp.float32
    )
    d_norm_mlp = lax.dot_general(
        d_up_low, up_full, contract_cols, preferred_element_type=jnp.float32
    )
    back_attn, gain_attn, shift_attn = norm_back(d_norm_attn, normal, inverse, attn_gain)
    back_mlp, gain_mlp, shift_mlp = norm_back(d_norm_mlp, normal, inverse, mlp_gain)
    input_grad = grad_out.astype(jnp.float32) + back_attn + back_mlp
    shard_rows = joined_weight.shape[0]
    shard_begin = lax.axis_index("fsdp") * shard_rows
    n_attn = lax.all_gather(norm_attn, "fsdp", axis=0, tiled=True)
    n_mlp = lax.all_gather(norm_mlp, "fsdp", axis=0, tiled=True)
    g_joined = lax.all_gather(d_joined_low, "fsdp", axis=0, tiled=True)
    g_up = lax.all_gather(d_up_low, "fsdp", axis=0, tiled=True)
    g_out = lax.all_gather(grad_out, "fsdp", axis=0, tiled=True)
    m_low = lax.all_gather(mix_low, "fsdp", axis=0, tiled=True)
    a_low = lax.all_gather(act_low, "fsdp", axis=0, tiled=True)
    cols_attn = lax.dynamic_slice_in_dim(n_attn, shard_begin, shard_rows, 1)
    cols_mlp = lax.dynamic_slice_in_dim(n_mlp, shard_begin, shard_rows, 1)
    out_cols = lax.dynamic_slice_in_dim(g_out, shard_begin, shard_rows, 1)
    dfused_weight, dup_weight, dattn_weight, ddown_weight = (
        lax.psum(
            lax.dot_general(
                cols_attn, g_joined, contract_rows, preferred_element_type=jnp.float32
            ).astype(jnp.bfloat16),
            "ctx",
        ).astype(jnp.float32),
        lax.psum(
            lax.dot_general(
                cols_mlp, g_up, contract_rows, preferred_element_type=jnp.float32
            ).astype(jnp.bfloat16),
            "ctx",
        ).astype(jnp.float32),
        lax.psum(
            lax.dot_general(
                m_low, out_cols, contract_rows, preferred_element_type=jnp.float32
            ).astype(jnp.bfloat16),
            "ctx",
        ).astype(jnp.float32),
        lax.psum(
            lax.dot_general(
                a_low, out_cols, contract_rows, preferred_element_type=jnp.float32
            ).astype(jnp.bfloat16),
            "ctx",
        ).astype(jnp.float32),
    )
    out_sum = jnp.sum(grad_out.astype(jnp.float32), 0)
    small = lax.psum(
        (
            gain_attn,
            shift_attn,
            gain_mlp,
            shift_mlp,
            jnp.sum(d_joined, 0),
            out_sum,
            jnp.sum(d_up, 0),
        ),
        ("ctx", "fsdp"),
    )
    return (
        layer_output[None],
        input_grad[None],
        small[0],
        small[1],
        small[2],
        small[3],
        dfused_weight,
        small[4],
        dattn_weight,
        small[5],
        dup_weight,
        small[6],
        ddown_weight,
        small[5],
    )


CHIPS = 4
DEPTH = 4
MESH = pl.DeviceIdType.MESH
VMEM_SPEC = pl.BlockSpec(memory_space=pltpu.VMEM)
ANY_SPEC = pl.BlockSpec(memory_space=pl.ANY)


def push(source, target, send_sem, recv_sem, **where):
    return pltpu.make_async_remote_copy(
        src_ref=source,
        dst_ref=target,
        send_sem=send_sem,
        recv_sem=recv_sem,
        device_id=where,
        device_id_type=MESH,
    )


def greet(count_ctx, me, other):
    barrier = pltpu.get_barrier_semaphore()
    for step in range(1, DEPTH):
        pl.semaphore_signal(
            barrier, inc=1, device_id={"fsdp": (other + step) % DEPTH}, device_id_type=MESH
        )
    for target in count_ctx:
        pl.semaphore_signal(barrier, inc=1, device_id={"ctx": target}, device_id_type=MESH)
    pl.semaphore_wait(barrier, DEPTH - 1 + len(count_ctx))


def gather_kernel(a_ref, b_ref, a_all, b_all, own_sem, zs, zr, cs, cr, ss, sr):
    me = lax.axis_index("ctx")
    depth = lax.axis_index("fsdp")
    core = me % 2
    chip = me // 2
    sibling = me + 1 - 2 * core
    greet([((chip + k) % CHIPS) * 2 + core for k in range(1, CHIPS)] + [sibling], me, depth)
    sends = []
    for k in range(1, CHIPS):
        target = ((chip + k) % CHIPS) * 2 + core
        sends.append(push(a_ref, a_all.at[me], cs.at[k - 1], cr.at[k - 1], ctx=target))
        sends.append(
            push(
                b_ref,
                b_all.at[depth],
                zs.at[k - 1],
                zr.at[k - 1],
                fsdp=(depth + k) % DEPTH,
            )
        )
    sends.append(push(a_ref, a_all.at[me], ss.at[0], sr.at[0], ctx=sibling))
    own = [
        pltpu.make_async_copy(a_ref, a_all.at[me], own_sem.at[0]),
        pltpu.make_async_copy(b_ref, b_all.at[depth], own_sem.at[1]),
    ]
    for copy in sends + own:
        copy.start()
    for k in range(1, CHIPS):
        source = ((chip + CHIPS - k) % CHIPS) * 2 + core
        block = a_all.at[source]
        push(block, block, cs.at[k - 1], cr.at[k - 1], ctx=sibling).wait_recv()
        onward = push(block, block, ss.at[k], sr.at[k], ctx=sibling)
        onward.start()
        sends.append(onward)
    for k in range(CHIPS):
        source = ((chip + CHIPS - k) % CHIPS) * 2 + 1 - core
        block = a_all.at[source]
        push(block, block, ss.at[k], sr.at[k], ctx=sibling).wait_recv()
    for k in range(1, DEPTH):
        block = b_all.at[(depth + DEPTH - k) % DEPTH]
        push(block, block, zs.at[k - 1], zr.at[k - 1], fsdp=depth).wait_recv()
    for copy in sends:
        copy.wait_send()
    for copy in own:
        copy.wait()


def gather_all(rows, weights):
    dma = pltpu.SemaphoreType.DMA
    return pl.pallas_call(
        gather_kernel,
        out_shape=(
            jax.ShapeDtypeStruct((2 * CHIPS,) + rows.shape, rows.dtype),
            jax.ShapeDtypeStruct((DEPTH,) + weights.shape, weights.dtype),
        ),
        in_specs=[ANY_SPEC] * 2,
        out_specs=(ANY_SPEC, ANY_SPEC),
        scratch_shapes=[dma((2,)), dma((3,)), dma((3,)), dma((3,)), dma((3,)), dma((4,)), dma((4,))],
        compiler_params=pltpu.CompilerParams(collective_id=1, has_side_effects=True),
    )(rows, weights)


PIECES = 4


def reduce_kernel(
    y_ref, w_ref, s_ref, y_out, w_all, s_out,
    pair, held, far, deep, small_z, small_c,
    pair_s, pair_r, far_s, far_r, zs, zr, cs, cr, ss, sr, sz_s, sz_r, sc_s, sc_r,
):
    me = lax.axis_index("ctx")
    depth = lax.axis_index("fsdp")
    core = me % 2
    chip = me // 2
    sibling = me + 1 - 2 * core
    context = 2 * CHIPS
    greet([(me + k) % context for k in range(1, context)], me, depth)
    part_rows = w_ref.shape[1] // PIECES
    sends = []

    def go(copy):
        copy.start()
        sends.append(copy)

    def peer(k):
        return ((chip + k) % CHIPS) * 2 + core

    def origin(k):
        return ((chip + CHIPS - k) % CHIPS) * 2 + core

    for k in range(1, DEPTH):
        target = (depth + k) % DEPTH
        go(push(s_ref, small_z.at[depth], sz_s.at[k - 1], sz_r.at[k - 1], fsdp=target))
    for k in (1, 2, 3, 0):
        block = ((chip + k) % CHIPS) * 2 + 1 - core
        go(push(y_ref.at[block], pair.at[k], pair_s.at[k], pair_r.at[k], ctx=sibling))
    for piece in range(PIECES):
        rows = pl.ds(piece * part_rows, part_rows)
        for k in range(1, DEPTH):
            target = (depth + k) % DEPTH
            go(
                push(
                    w_ref.at[target, rows],
                    deep.at[k - 1, rows],
                    zs.at[piece, k - 1],
                    zr.at[piece, k - 1],
                    fsdp=target,
                )
            )
    for k in (1, 2, 3, 0):
        push(pair.at[k], pair.at[k], pair_s.at[k], pair_r.at[k], ctx=sibling).wait_recv()
        joint = y_ref[peer(k)].astype(jnp.float32) + pair[k].astype(jnp.float32)
        if k:
            held[k - 1] = joint.astype(jnp.bfloat16)
            go(push(held.at[k - 1], far.at[k - 1], far_s.at[k - 1], far_r.at[k - 1], ctx=peer(k)))
        else:
            y_out[...] = joint
    small_z[depth] = s_ref[...]
    for k in range(1, DEPTH):
        slot = small_z.at[(depth + DEPTH - k) % DEPTH]
        push(slot, slot, sz_s.at[k - 1], sz_r.at[k - 1], fsdp=depth).wait_recv()
    small_c[me] = (small_z[0] + small_z[1]) + (small_z[2] + small_z[3])
    for k in range(1, context):
        slot = small_c.at[me]
        go(push(slot, slot, sc_s.at[k - 1], sc_r.at[k - 1], ctx=(me + k) % context))

    def hand_on(piece):
        rows = pl.ds(piece * part_rows, part_rows)
        for k in range(1, CHIPS):
            block = w_all.at[origin(k), rows]
            push(block, block, cs.at[piece, k - 1], cr.at[piece, k - 1], ctx=sibling).wait_recv()
            go(push(block, block, ss.at[piece, k], sr.at[piece, k], ctx=sibling))

    for piece in range(PIECES):
        rows = pl.ds(piece * part_rows, part_rows)
        total = w_ref[depth, rows].astype(jnp.float32)
        for k in range(1, DEPTH):
            slot = deep.at[k - 1, rows]
            push(slot, slot, zs.at[piece, k - 1], zr.at[piece, k - 1], fsdp=depth).wait_recv()
            total = total + deep[k - 1, rows].astype(jnp.float32)
        w_all[me, rows] = total.astype(jnp.bfloat16)
        block = w_all.at[me, rows]
        for k in range(1, CHIPS):
            go(push(block, block, cs.at[piece, k - 1], cr.at[piece, k - 1], ctx=peer(k)))
        go(push(block, block, ss.at[piece, 0], sr.at[piece, 0], ctx=sibling))
        if piece:
            hand_on(piece - 1)
    for k in range(1, CHIPS):
        slot = far.at[k - 1]
        push(slot, slot, far_s.at[k - 1], far_r.at[k - 1], ctx=sibling).wait_recv()
        y_out[...] += far[k - 1].astype(jnp.float32)
    for k in range(1, context):
        slot = small_c.at[(me + context - k) % context]
        push(slot, slot, sc_s.at[k - 1], sc_r.at[k - 1], ctx=sibling).wait_recv()
    total = small_c[0]
    for k in range(1, context):
        total = total + small_c[k]
    s_out[...] = total
    hand_on(PIECES - 1)
    for piece in range(PIECES):
        rows = pl.ds(piece * part_rows, part_rows)
        for k in range(CHIPS):
            block = w_all.at[((chip + CHIPS - k) % CHIPS) * 2 + 1 - core, rows]
            push(block, block, ss.at[piece, k], sr.at[piece, k], ctx=sibling).wait_recv()
    for copy in sends:
        copy.wait_send()


def reduce_all(partial, weight_grads, small):
    context, rows, columns = partial.shape
    dma = pltpu.SemaphoreType.DMA
    return pl.pallas_call(
        reduce_kernel,
        out_shape=(
            jax.ShapeDtypeStruct((rows, columns), jnp.float32),
            jax.ShapeDtypeStruct((context,) + weight_grads.shape[1:], jnp.bfloat16),
            jax.ShapeDtypeStruct(small.shape, jnp.float32),
        ),
        in_specs=[VMEM_SPEC] * 3,
        out_specs=(VMEM_SPEC,) * 3,
        scratch_shapes=[
            pltpu.VMEM((CHIPS, rows, columns), jnp.bfloat16),
            pltpu.VMEM((CHIPS - 1, rows, columns), jnp.bfloat16),
            pltpu.VMEM((CHIPS - 1, rows, columns), jnp.bfloat16),
            pltpu.VMEM((DEPTH - 1,) + weight_grads.shape[1:], jnp.bfloat16),
            pltpu.VMEM((DEPTH,) + small.shape, jnp.float32),
            pltpu.VMEM((context,) + small.shape, jnp.float32),
        ]
        + [dma((4,)), dma((4,)), dma((3,)), dma((3,))]
        + [dma((PIECES, 3))] * 4
        + [dma((PIECES, 4))] * 2
        + [dma((3,)), dma((3,)), dma((7,)), dma((7,))],
        compiler_params=pltpu.CompilerParams(
            collective_id=2, has_side_effects=True, vmem_limit_bytes=40 * 1024 * 1024
        ),
    )(partial, weight_grads, small)


Q_TILE = 256
PAIR = 2 * HEAD


def attention_kernel(
    joined_ref, dmix_ref, cos_ref, down_ref, up_ref, q_pl, q_low, k_pl,
    mix_ref, grad_ref, bias_ref, q_s, k_s, v_s, g_s, dk_s, dv_s,
):
    length = joined_ref.shape[0]
    scale = HEAD ** (-0.5)
    half = ROT // 2
    dot = lambda a, b, dims: lax.dot_general(a, b, dims, preferred_element_type=jnp.float32)
    contract_inner = (((1,), (0,)), ((), ()))

    def turn(block, sign):
        return (
            block * cos_ref[...]
            + pltpu.roll(block, PAIR - half, 1) * (sign * down_ref[...])
            + pltpu.roll(block, half, 1) * (sign * up_ref[...])
        )

    query = turn(joined_ref[:, :PAIR], 1.0)
    key = turn(joined_ref[:, PAIR : 2 * PAIR], 1.0)
    value = joined_ref[:, 2 * PAIR :]
    mix_grad = dmix_ref[...].astype(jnp.float32)
    lane = lax.broadcasted_iota(jnp.int32, (1, PAIR), 1)
    for head in range(2):
        own = (lane // HEAD) == head
        q_s[head] = jnp.where(own, query, 0.0).astype(jnp.bfloat16)
        k_s[head] = jnp.where(own, key, 0.0).astype(jnp.bfloat16)
        v_s[head] = jnp.where(own, value, 0.0).astype(jnp.bfloat16)
        g_s[head] = jnp.where(own, mix_grad, 0.0).astype(jnp.bfloat16)
    dk_s[...] = jnp.zeros_like(dk_s)
    dv_s[...] = jnp.zeros_like(dv_s)
    key_place = k_pl[...]
    dq_parts = []
    for tile in range(length // Q_TILE):
        rows = slice(tile * Q_TILE, (tile + 1) * Q_TILE)
        valid = (key_place <= q_pl[rows, :]) & (key_place >= q_low[rows, :])
        mixed = jnp.zeros((Q_TILE, PAIR), jnp.float32)
        d_query = jnp.zeros((Q_TILE, PAIR), jnp.float32)
        for head in range(2):
            q_t = q_s[head, rows, :]
            g_t = g_s[head, rows, :]
            score = jnp.where(valid, dot(q_t, k_s[head], contract_cols) * scale, masked_score)
            top = jnp.max(score, -1, keepdims=True)
            weight = jnp.exp(score - top)
            prob = weight * (1.0 / jnp.sum(weight, -1, keepdims=True))
            prob_low = prob.astype(jnp.bfloat16)
            mix_h = dot(prob_low, v_s[head], contract_inner)
            delta = jnp.sum(g_t.astype(jnp.float32) * mix_h, -1, keepdims=True)
            d_prob = dot(g_t, v_s[head], contract_cols)
            d_score = (prob * (d_prob - delta)).astype(jnp.bfloat16)
            d_query += dot(d_score, k_s[head], contract_inner)
            dk_s[...] += dot(d_score, q_t, contract_rows)
            dv_s[...] += dot(prob_low, g_t, contract_rows)
            mixed += mix_h
        mix_ref[rows, :] = mixed.astype(jnp.bfloat16)
        dq_parts.append(d_query)
    d_q = turn(jnp.concatenate(dq_parts, 0) * scale, -1.0)
    d_k = turn(dk_s[...] * scale, -1.0)
    for index, block in enumerate((d_q, d_k, dv_s[...])):
        columns = slice(index * PAIR, (index + 1) * PAIR)
        grad_ref[:, columns] = block.astype(jnp.bfloat16)
        bias_ref[:, columns] = jnp.sum(block, 0, keepdims=True)


def attention(joined, d_mix, tables, places, lowest):
    length = joined.shape[0]
    keep = [pltpu.VMEM((2, length, PAIR), jnp.bfloat16)] * 4
    return pl.pallas_call(
        attention_kernel,
        out_shape=(
            jax.ShapeDtypeStruct((length, PAIR), jnp.bfloat16),
            jax.ShapeDtypeStruct((length, 3 * PAIR), jnp.bfloat16),
            jax.ShapeDtypeStruct((1, 3 * PAIR), jnp.float32),
        ),
        in_specs=[VMEM_SPEC] * 8,
        out_specs=(VMEM_SPEC,) * 3,
        scratch_shapes=keep + [pltpu.VMEM((length, PAIR), jnp.float32)] * 2,
        compiler_params=pltpu.CompilerParams(vmem_limit_bytes=48 * 1024 * 1024),
    )(joined, d_mix, *tables, places[:, None], lowest[:, None], places[None, :])


def split_local(
    layer_input,
    cotangent,
    block_order,
    boundary,
    attn_gain,
    attn_shift,
    mlp_gain,
    mlp_shift,
    joined_weight,
    joined_bias,
    attn_weight,
    attn_bias,
    up_weight,
    up_bias,
    down_weight,
    down_bias,
):
    rows = layer_input.shape[1]
    width = layer_input.shape[2]
    context = 2 * CHIPS
    length = rows * context
    half = rows // 2
    holders = HEADS // 2
    shard = joined_weight.shape[0]
    units = up_weight.shape[1] // context
    me = lax.axis_index("ctx")
    slot = jnp.minimum(me, holders - 1)
    holds = me < holders

    own_joined = lax.dynamic_slice(
        joined_weight.reshape(shard, 3, width), (0, 0, slot * PAIR), (shard, 3, PAIR)
    ).reshape(shard, 3 * PAIR)
    own_attn = lax.dynamic_slice(attn_weight, (slot * PAIR, 0), (PAIR, shard)).T
    own_up = lax.dynamic_slice(up_weight, (0, me * units), (shard, units))
    own_down = lax.dynamic_slice(down_weight, (me * units, 0), (units, shard)).T
    own_weights = jnp.concatenate(
        [
            jnp.where(holds, own_joined, 0),
            own_up,
            own_down,
            jnp.where(holds, own_attn, 0),
        ],
        1,
    )
    own_rows = jnp.concatenate([layer_input[0], cotangent[0]], 1)
    rows_all, weights_all = gather_all(own_rows, own_weights)
    rows_all = rows_all.reshape(length, 2 * width)
    weights_all = weights_all.reshape(width, -1)
    w_joined = weights_all[:, : 3 * PAIR]
    w_up = weights_all[:, 3 * PAIR : 3 * PAIR + units]
    w_out = weights_all[:, 3 * PAIR + units :]
    hidden = rows_all[:, :width].astype(jnp.float32)
    grad_out = rows_all[:, width:]
    b_joined = jnp.where(
        holds,
        lax.dynamic_slice(joined_bias.reshape(3, width), (0, slot * PAIR), (3, PAIR)),
        0.0,
    ).reshape(3 * PAIR)
    b_up = lax.dynamic_slice(up_bias, (me * units,), (units,))

    places = place_lookup(block_order, jnp.int32(0), length, half)
    lowest = jnp.where(places >= boundary[0], boundary[0], 0)
    lane = jnp.arange(PAIR, dtype=jnp.int32) % HEAD
    bend = ROT // 2
    freq = 10000.0 ** (-2.0 * (lane % bend).astype(jnp.float32) / ROT)
    angles = places.astype(jnp.float32)[:, None] * freq[None, :]
    cosine = jnp.where(lane < ROT, jnp.cos(angles), 1.0)
    sine = jnp.sin(angles)
    tables = (
        cosine,
        jnp.where(lane < bend, -sine, 0.0),
        jnp.where((lane >= bend) & (lane < ROT), sine, 0.0),
    )

    normal, _ = normalize_parts(hidden)
    norm_attn = (normal * attn_gain + attn_shift).astype(jnp.bfloat16)
    norm_mlp = (normal * mlp_gain + mlp_shift).astype(jnp.bfloat16)
    joined = jnp.dot(norm_attn, w_joined, preferred_element_type=jnp.float32) + b_joined
    upper = jnp.dot(norm_mlp, w_up, preferred_element_type=jnp.float32) + b_up
    d_out = jnp.dot(grad_out, w_out, preferred_element_type=jnp.float32)
    d_act = d_out[:, :units]
    d_mix = d_out[:, units:].astype(jnp.bfloat16)
    mix_low, d_joined_low, joined_sums = attention(joined, d_mix, tables, places, lowest)
    act, gelu_pull = jax.vjp(lambda argument: jax.nn.gelu(argument, approximate=False), upper)
    d_up = gelu_pull(d_act)[0]
    d_up_low = d_up.astype(jnp.bfloat16)
    outer = jnp.concatenate([act.astype(jnp.bfloat16), mix_low], 1)
    branches = lax.dot_general(outer, w_out, contract_cols, preferred_element_type=jnp.float32)
    d_norm_attn = lax.dot_general(
        d_joined_low, w_joined, contract_cols, preferred_element_type=jnp.float32
    )
    d_norm_mlp = lax.dot_general(d_up_low, w_up, contract_cols, preferred_element_type=jnp.float32)
    scaled = d_norm_attn * attn_gain + d_norm_mlp * mlp_gain
    partial = jnp.concatenate([branches, scaled], 1).astype(jnp.bfloat16)
    weight_grads = jnp.concatenate(
        [
            lax.dot_general(norm_attn, d_joined_low, contract_rows, preferred_element_type=jnp.float32),
            lax.dot_general(norm_mlp, d_up_low, contract_rows, preferred_element_type=jnp.float32),
            lax.dot_general(grad_out, outer, contract_rows, preferred_element_type=jnp.float32),
        ],
        1,
    ).astype(jnp.bfloat16)
    mine = jnp.arange(context, dtype=jnp.int32) == me
    spread_joined = jnp.where(
        mine[:holders][None, :, None], joined_sums.reshape(3, 1, PAIR), 0.0
    ).reshape(-1)
    spread_up = jnp.where(mine[:, None], jnp.sum(d_up, 0)[None, :], 0.0).reshape(-1)
    small = jnp.concatenate(
        [
            jnp.sum(d_norm_attn * normal, 0),
            jnp.sum(d_norm_attn, 0),
            jnp.sum(d_norm_mlp * normal, 0),
            jnp.sum(d_norm_mlp, 0),
            spread_joined,
            jnp.sum(cotangent[0].astype(jnp.float32), 0),
            spread_up,
        ]
    )
    sums, grads, small = reduce_all(
        partial.reshape(context, rows, 2 * width),
        weight_grads.reshape(DEPTH, shard, -1),
        small.reshape(-1, 128),
    )
    small = small.reshape(-1)
    own_hidden = layer_input[0].astype(jnp.float32)
    layer_output = (own_hidden + sums[:, :width] + attn_bias + down_bias).astype(jnp.bfloat16)
    own_normal, own_inverse = normalize_parts(own_hidden)
    inner = sums[:, width:]
    back = own_inverse * (
        inner
        - jnp.mean(inner, -1, keepdims=True)
        - own_normal * jnp.mean(inner * own_normal, -1, keepdims=True)
    )
    input_grad = cotangent[0].astype(jnp.float32) + back
    ends = (3 * PAIR, 3 * PAIR + units, 3 * PAIR + 2 * units)
    dfused = (
        grads[:holders, :, : ends[0]]
        .reshape(holders, shard, 3, PAIR)
        .transpose(1, 2, 0, 3)
        .reshape(shard, 3 * width)
        .astype(jnp.float32)
    )
    dup = grads[:, :, ends[0] : ends[1]].transpose(1, 0, 2).reshape(shard, -1).astype(jnp.float32)
    ddown = grads[:, :, ends[1] : ends[2]].transpose(0, 2, 1).reshape(-1, shard).astype(jnp.float32)
    dattn = grads[:holders, :, ends[2] :].transpose(0, 2, 1).reshape(width, shard)
    base = 4 * width
    fused_end = base + 3 * width
    out_end = fused_end + width
    return (
        layer_output[None],
        input_grad[None],
        small[:width],
        small[width : 2 * width],
        small[2 * width : 3 * width],
        small[3 * width : base],
        dfused,
        small[base:fused_end],
        dattn.astype(jnp.float32),
        small[fused_end:out_end],
        dup,
        small[out_end:],
        ddown,
        small[fused_end:out_end],
    )


def solution(mesh):
    split = mesh.shape["ctx"] == 2 * CHIPS and mesh.shape["fsdp"] == DEPTH
    return jax.shard_map(
        split_local if split else local,
        mesh=mesh,
        in_specs=(
            P("fsdp", "ctx", None),
            P("fsdp", "ctx", None),
            P(),
            P("fsdp"),
            P(),
            P(),
            P(),
            P(),
            P("fsdp", None),
            P(),
            P(None, "fsdp"),
            P(),
            P("fsdp", None),
            P(),
            P(None, "fsdp"),
            P(),
        ),
        out_specs=(
            P("fsdp", "ctx", None),
            P("fsdp", "ctx", None),
            P(),
            P(),
            P(),
            P(),
            P("fsdp", None),
            P(),
            P(None, "fsdp"),
            P(),
            P("fsdp", None),
            P(),
            P(None, "fsdp"),
            P(),
        ),
        check_vma=False,
    )
```

```python
import jax
import jax.numpy as jnp
from jax import lax
from jax.experimental import pallas as pl
from jax.experimental.pallas import tpu as pltpu
from jax.sharding import PartitionSpec as P

HEADS = 12
HEAD = 64
ROT = 16


epsilon = 1e-05
masked_score = -1e30
contract_rows = (((0,), (0,)), ((), ()))
contract_cols = (((1,), (1,)), ((), ()))


def place_lookup(block_order, begin, count, half):
    storage = begin + jnp.arange(count, dtype=jnp.int32)
    slots = storage // half
    table = jnp.arange(block_order.shape[0], dtype=jnp.int32)
    chosen = jnp.sum(jnp.where(slots[:, None] == table[None, :], block_order[None, :], 0), axis=1)
    return chosen * half + storage % half


def normalize_parts(value):
    average = jnp.mean(value, -1, keepdims=True)
    centered = value - average
    inverse = lax.rsqrt(jnp.mean(centered * centered, -1, keepdims=True) + epsilon)
    return (centered * inverse, inverse)


def norm_back(d_norm, normal, inverse, gain):
    scaled = d_norm * gain
    inner = (
        scaled
        - jnp.mean(scaled, -1, keepdims=True)
        - normal * jnp.mean(scaled * normal, -1, keepdims=True)
    )
    return (inner * inverse, jnp.sum(d_norm * normal, 0), jnp.sum(d_norm, 0))


def rotary_tables(places):
    half = ROT // 2
    freq = 10000.0 ** (-2.0 * jnp.arange(half, dtype=jnp.float32) / ROT)
    angles = places.astype(jnp.float32)[:, None] * freq[None, :]
    return (jnp.cos(angles)[:, None, :], jnp.sin(angles)[:, None, :])


def rotate(tensor, cosine, sine):
    half = ROT // 2
    first = tensor[..., :half]
    second = tensor[..., half:ROT]
    return jnp.concatenate(
        [first * cosine - second * sine, second * cosine + first * sine, tensor[..., ROT:]], -1
    )


def rotate_back(tensor, cosine, sine):
    half = ROT // 2
    first = tensor[..., :half]
    second = tensor[..., half:ROT]
    return jnp.concatenate(
        [first * cosine + second * sine, second * cosine - first * sine, tensor[..., ROT:]], -1
    )


def pair_terms(
    query_heads,
    query_pl,
    query_dc,
    mix_grad,
    log_total,
    delta_rows,
    key_heads,
    value_heads,
    key_pl,
    key_dc,
    scale,
):
    scores = (
        jnp.einsum("qhd,khd->hqk", query_heads, key_heads, preferred_element_type=jnp.float32)
        * scale
    )
    valid = ((key_pl[None, :] <= query_pl[:, None]) & (key_dc[None, :] == query_dc[:, None]))[None]
    scores = jnp.where(valid, scores, masked_score)
    prob = jnp.where(valid, jnp.exp(scores - log_total[..., None]), 0.0)
    d_prob = jnp.einsum("qhd,khd->hqk", mix_grad, value_heads, preferred_element_type=jnp.float32)
    d_score = (prob * (d_prob - delta_rows[..., None])).astype(jnp.bfloat16)
    return (prob, d_score)


def local(
    layer_input,
    cotangent,
    block_order,
    boundary,
    attn_gain,
    attn_shift,
    mlp_gain,
    mlp_shift,
    joined_weight,
    joined_bias,
    attn_weight,
    attn_bias,
    up_weight,
    up_bias,
    down_weight,
    down_bias,
):
    local_rows = layer_input.shape[1]
    width = layer_input.shape[2]
    context = lax.axis_size("ctx")
    length = local_rows * context
    half = local_rows // 2
    blocks = 2 * context
    key_tile = min(512, length)
    tiles_all = length // key_tile
    scale = HEAD ** (-0.5)
    cutoff = boundary[0]
    hidden = layer_input[0].astype(jnp.float32)
    grad_out = cotangent[0]
    my_index = lax.axis_index("ctx")
    begin = my_index * local_rows
    query_places = place_lookup(block_order, begin, local_rows, half)
    query_docs = (query_places >= cutoff).astype(jnp.int32)
    cosine, sine = rotary_tables(query_places)
    table = jnp.arange(blocks, dtype=jnp.int32)
    inverse_order = jnp.sum(
        jnp.where(block_order[None, :] == table[:, None], table[None, :], 0), axis=1
    )

    def place_order(whole):
        columns = whole.shape[1]
        return jnp.take(whole.reshape(blocks, half, columns), inverse_order, axis=0).reshape(
            length, columns
        )

    def block_first(index):
        return lax.dynamic_index_in_dim(block_order, 2 * my_index + index, 0, keepdims=False) * half

    normal, inverse = normalize_parts(hidden)
    norm_attn = (normal * attn_gain + attn_shift).astype(jnp.bfloat16)
    norm_mlp = (normal * mlp_gain + mlp_shift).astype(jnp.bfloat16)
    joined_full, up_full = (
        lax.all_gather(joined_weight, "fsdp", axis=0, tiled=True),
        lax.all_gather(up_weight, "fsdp", axis=0, tiled=True),
    )
    attn_full, down_full = (
        lax.all_gather(attn_weight, "fsdp", axis=1, tiled=True),
        lax.all_gather(down_weight, "fsdp", axis=1, tiled=True),
    )
    joined_lin = jnp.dot(norm_attn, joined_full, preferred_element_type=jnp.float32)
    up_lin = jnp.dot(norm_mlp, up_full, preferred_element_type=jnp.float32)
    joined = joined_lin + joined_bias
    queries = (
        rotate(joined[:, :width].reshape(local_rows, HEADS, HEAD), cosine, sine)
        .astype(jnp.bfloat16)
        .reshape(local_rows, width)
    )
    keys = (
        rotate(joined[:, width : 2 * width].reshape(local_rows, HEADS, HEAD), cosine, sine)
        .astype(jnp.bfloat16)
        .reshape(local_rows, width)
    )
    values = joined[:, 2 * width :].astype(jnp.bfloat16)
    kv_whole = lax.all_gather(jnp.concatenate([keys, values], 1), "ctx", axis=0, tiled=True)
    kv_ordered = place_order(kv_whole)

    def key_block_at(index):
        start = index * key_tile
        block = lax.dynamic_slice_in_dim(kv_ordered, start, key_tile, 0)
        key_pl = start + jnp.arange(key_tile, dtype=jnp.int32)
        key_dc = (key_pl >= cutoff).astype(jnp.int32)
        return (
            block[:, :width].reshape(key_tile, HEADS, HEAD),
            block[:, width:].reshape(key_tile, HEADS, HEAD),
            key_pl,
            key_dc,
        )

    mixtures = []
    tops = []
    totals = []
    for part in range(2):
        q_heads = queries[part * half : (part + 1) * half].reshape(half, HEADS, HEAD)
        q_pl = query_places[part * half : (part + 1) * half]
        q_dc = query_docs[part * half : (part + 1) * half]
        reach = (block_first(part) + half + key_tile - 1) // key_tile

        def forward_step(index, state, q_heads=q_heads, q_pl=q_pl, q_dc=q_dc):
            mixture, top, total = state
            key_heads, value_heads, key_pl, key_dc = key_block_at(index)
            scores = (
                jnp.einsum("qhd,khd->hqk", q_heads, key_heads, preferred_element_type=jnp.float32)
                * scale
            )
            valid = ((key_pl[None, :] <= q_pl[:, None]) & (key_dc[None, :] == q_dc[:, None]))[None]
            scores = jnp.where(valid, scores, masked_score)
            new_top = jnp.maximum(top, jnp.max(scores, -1))
            weights = jnp.where(valid, jnp.exp(scores - new_top[..., None]), 0.0)
            factor = jnp.exp(top - new_top)
            total = total * factor + jnp.sum(weights, -1)
            mixture = mixture * factor.T[:, :, None] + jnp.einsum(
                "hqk,khd->qhd",
                weights.astype(jnp.bfloat16),
                value_heads,
                preferred_element_type=jnp.float32,
            )
            return (mixture, new_top, total)

        start_state = (
            jnp.zeros((half, HEADS, HEAD), jnp.float32),
            jnp.full((HEADS, half), masked_score, jnp.float32),
            jnp.zeros((HEADS, half), jnp.float32),
        )
        mixture, top, total = lax.fori_loop(jnp.int32(0), reach, forward_step, start_state)
        mixtures.append(mixture)
        tops.append(top)
        totals.append(total)
    mixture = jnp.concatenate(mixtures, 0)
    top = jnp.concatenate(tops, 1)
    total = jnp.concatenate(totals, 1)
    logsum = top + jnp.log(total)
    mixed = mixture / total.T[:, :, None]
    mix_low = mixed.reshape(local_rows, width).astype(jnp.bfloat16)
    upper = up_lin + up_bias
    act, gelu_pull = jax.vjp(lambda argument: jax.nn.gelu(argument, approximate=False), upper)
    act_low = act.astype(jnp.bfloat16)
    branches = jnp.dot(mix_low, attn_full, preferred_element_type=jnp.float32) + jnp.dot(
        act_low, down_full, preferred_element_type=jnp.float32
    )
    layer_output = (hidden + branches + attn_bias + down_bias).astype(jnp.bfloat16)
    d_attn = lax.dot_general(grad_out, attn_full, contract_cols, preferred_element_type=jnp.float32)
    d_act = lax.dot_general(grad_out, down_full, contract_cols, preferred_element_type=jnp.float32)
    d_mix_flat = d_attn.astype(jnp.bfloat16)
    d_mix = d_mix_flat.reshape(local_rows, HEADS, HEAD)
    delta = jnp.einsum("qhd,qhd->hq", d_mix.astype(jnp.float32), mixed)
    d_up = gelu_pull(d_act)[0]
    d_up_low = d_up.astype(jnp.bfloat16)
    query_grads = []
    for part in range(2):
        q_heads = queries[part * half : (part + 1) * half].reshape(half, HEADS, HEAD)
        q_pl = query_places[part * half : (part + 1) * half]
        q_dc = query_docs[part * half : (part + 1) * half]
        g_heads = d_mix[part * half : (part + 1) * half]
        log_rows = logsum[:, part * half : (part + 1) * half]
        delta_part = delta[:, part * half : (part + 1) * half]
        reach = (block_first(part) + half + key_tile - 1) // key_tile

        def query_step(
            index,
            d_query,
            q_heads=q_heads,
            q_pl=q_pl,
            q_dc=q_dc,
            g_heads=g_heads,
            log_rows=log_rows,
            delta_part=delta_part,
        ):
            key_heads, value_heads, key_pl, key_dc = key_block_at(index)
            prob, d_score = pair_terms(
                q_heads,
                q_pl,
                q_dc,
                g_heads,
                log_rows,
                delta_part,
                key_heads,
                value_heads,
                key_pl,
                key_dc,
                scale,
            )
            return (
                d_query
                + jnp.einsum("hqk,khd->qhd", d_score, key_heads, preferred_element_type=jnp.float32)
                * scale
            )

        query_grads.append(
            lax.fori_loop(
                jnp.int32(0), reach, query_step, jnp.zeros((half, HEADS, HEAD), jnp.float32)
            )
        )
    d_query = jnp.concatenate(query_grads, 0)
    packed_whole = lax.all_gather(
        jnp.concatenate([queries, d_mix_flat], 1), "ctx", axis=0, tiled=True
    )
    stats_whole = lax.all_gather(jnp.concatenate([logsum.T, delta.T], 1), "ctx", axis=0, tiled=True)
    packed_ordered = place_order(packed_whole)
    stats_ordered = place_order(stats_whole)
    key_grads = []
    value_grads = []
    for part in range(2):
        own_keys = keys[part * half : (part + 1) * half].reshape(half, HEADS, HEAD)
        own_values = values[part * half : (part + 1) * half].reshape(half, HEADS, HEAD)
        own_pl = query_places[part * half : (part + 1) * half]
        own_dc = query_docs[part * half : (part + 1) * half]
        first_tile = block_first(part) // key_tile

        def owner_step(
            index, state, own_keys=own_keys, own_values=own_values, own_pl=own_pl, own_dc=own_dc
        ):
            start = index * key_tile
            block = lax.dynamic_slice_in_dim(packed_ordered, start, key_tile, 0)
            stat_block = lax.dynamic_slice_in_dim(stats_ordered, start, key_tile, 0)
            q_heads = block[:, :width].reshape(key_tile, HEADS, HEAD)
            g_heads = block[:, width:].reshape(key_tile, HEADS, HEAD)
            q_pl = start + jnp.arange(key_tile, dtype=jnp.int32)
            q_dc = (q_pl >= cutoff).astype(jnp.int32)
            prob, d_score = pair_terms(
                q_heads,
                q_pl,
                q_dc,
                g_heads,
                stat_block[:, :HEADS].T,
                stat_block[:, HEADS:].T,
                own_keys,
                own_values,
                own_pl,
                own_dc,
                scale,
            )
            d_key = (
                jnp.einsum("hqk,qhd->khd", d_score, q_heads, preferred_element_type=jnp.float32)
                * scale
            )
            d_value = jnp.einsum(
                "hqk,qhd->khd",
                prob.astype(jnp.bfloat16),
                g_heads,
                preferred_element_type=jnp.float32,
            )
            return (state[0] + d_key, state[1] + d_value)

        zero_heads = jnp.zeros((half, HEADS, HEAD), jnp.float32)
        part_key, part_value = lax.fori_loop(
            first_tile, jnp.int32(tiles_all), owner_step, (zero_heads, zero_heads)
        )
        key_grads.append(part_key)
        value_grads.append(part_value)
    key_grad_heads = jnp.concatenate(key_grads, 0)
    value_grad_rows = jnp.concatenate(value_grads, 0).reshape(local_rows, width)
    d_joined = jnp.concatenate(
        [
            rotate_back(d_query, cosine, sine).reshape(local_rows, width),
            rotate_back(key_grad_heads, cosine, sine).reshape(local_rows, width),
            value_grad_rows,
        ],
        1,
    )
    d_joined_low = d_joined.astype(jnp.bfloat16)
    d_norm_attn = lax.dot_general(
        d_joined_low, joined_full, contract_cols, preferred_element_type=jnp.float32
    )
    d_norm_mlp = lax.dot_general(
        d_up_low, up_full, contract_cols, preferred_element_type=jnp.float32
    )
    back_attn, gain_attn, shift_attn = norm_back(d_norm_attn, normal, inverse, attn_gain)
    back_mlp, gain_mlp, shift_mlp = norm_back(d_norm_mlp, normal, inverse, mlp_gain)
    input_grad = grad_out.astype(jnp.float32) + back_attn + back_mlp
    shard_rows = joined_weight.shape[0]
    shard_begin = lax.axis_index("fsdp") * shard_rows
    n_attn = lax.all_gather(norm_attn, "fsdp", axis=0, tiled=True)
    n_mlp = lax.all_gather(norm_mlp, "fsdp", axis=0, tiled=True)
    g_joined = lax.all_gather(d_joined_low, "fsdp", axis=0, tiled=True)
    g_up = lax.all_gather(d_up_low, "fsdp", axis=0, tiled=True)
    g_out = lax.all_gather(grad_out, "fsdp", axis=0, tiled=True)
    m_low = lax.all_gather(mix_low, "fsdp", axis=0, tiled=True)
    a_low = lax.all_gather(act_low, "fsdp", axis=0, tiled=True)
    cols_attn = lax.dynamic_slice_in_dim(n_attn, shard_begin, shard_rows, 1)
    cols_mlp = lax.dynamic_slice_in_dim(n_mlp, shard_begin, shard_rows, 1)
    out_cols = lax.dynamic_slice_in_dim(g_out, shard_begin, shard_rows, 1)
    dfused_weight, dup_weight, dattn_weight, ddown_weight = (
        lax.psum(
            lax.dot_general(
                cols_attn, g_joined, contract_rows, preferred_element_type=jnp.float32
            ).astype(jnp.bfloat16),
            "ctx",
        ).astype(jnp.float32),
        lax.psum(
            lax.dot_general(
                cols_mlp, g_up, contract_rows, preferred_element_type=jnp.float32
            ).astype(jnp.bfloat16),
            "ctx",
        ).astype(jnp.float32),
        lax.psum(
            lax.dot_general(
                m_low, out_cols, contract_rows, preferred_element_type=jnp.float32
            ).astype(jnp.bfloat16),
            "ctx",
        ).astype(jnp.float32),
        lax.psum(
            lax.dot_general(
                a_low, out_cols, contract_rows, preferred_element_type=jnp.float32
            ).astype(jnp.bfloat16),
            "ctx",
        ).astype(jnp.float32),
    )
    out_sum = jnp.sum(grad_out.astype(jnp.float32), 0)
    small = lax.psum(
        (
            gain_attn,
            shift_attn,
            gain_mlp,
            shift_mlp,
            jnp.sum(d_joined, 0),
            out_sum,
            jnp.sum(d_up, 0),
        ),
        ("ctx", "fsdp"),
    )
    return (
        layer_output[None],
        input_grad[None],
        small[0],
        small[1],
        small[2],
        small[3],
        dfused_weight,
        small[4],
        dattn_weight,
        small[5],
        dup_weight,
        small[6],
        ddown_weight,
        small[5],
    )


CHIPS = 4
DEPTH = 4
MESH = pl.DeviceIdType.MESH
VMEM_SPEC = pl.BlockSpec(memory_space=pltpu.VMEM)
ANY_SPEC = pl.BlockSpec(memory_space=pl.ANY)


def push(source, target, send_sem, recv_sem, **where):
    return pltpu.make_async_remote_copy(
        src_ref=source,
        dst_ref=target,
        send_sem=send_sem,
        recv_sem=recv_sem,
        device_id=where,
        device_id_type=MESH,
    )


def greet(count_ctx, me, other):
    barrier = pltpu.get_barrier_semaphore()
    for step in range(1, DEPTH):
        pl.semaphore_signal(
            barrier, inc=1, device_id={"fsdp": (other + step) % DEPTH}, device_id_type=MESH
        )
    for target in count_ctx:
        pl.semaphore_signal(barrier, inc=1, device_id={"ctx": target}, device_id_type=MESH)
    pl.semaphore_wait(barrier, DEPTH - 1 + len(count_ctx))


def gather_kernel(a_ref, b_ref, a_all, b_all, own_sem, zs, zr, cs, cr, ss, sr):
    me = lax.axis_index("ctx")
    depth = lax.axis_index("fsdp")
    core = me % 2
    chip = me // 2
    sibling = me + 1 - 2 * core
    greet([((chip + k) % CHIPS) * 2 + core for k in range(1, CHIPS)] + [sibling], me, depth)
    sends = []
    for k in range(1, CHIPS):
        target = ((chip + k) % CHIPS) * 2 + core
        sends.append(push(a_ref, a_all.at[me], cs.at[k - 1], cr.at[k - 1], ctx=target))
        sends.append(
            push(
                b_ref,
                b_all.at[depth],
                zs.at[k - 1],
                zr.at[k - 1],
                fsdp=(depth + k) % DEPTH,
            )
        )
    sends.append(push(a_ref, a_all.at[me], ss.at[0], sr.at[0], ctx=sibling))
    own = [
        pltpu.make_async_copy(a_ref, a_all.at[me], own_sem.at[0]),
        pltpu.make_async_copy(b_ref, b_all.at[depth], own_sem.at[1]),
    ]
    for copy in sends + own:
        copy.start()
    for k in range(1, CHIPS):
        source = ((chip + CHIPS - k) % CHIPS) * 2 + core
        block = a_all.at[source]
        push(block, block, cs.at[k - 1], cr.at[k - 1], ctx=sibling).wait_recv()
        onward = push(block, block, ss.at[k], sr.at[k], ctx=sibling)
        onward.start()
        sends.append(onward)
    for k in range(CHIPS):
        source = ((chip + CHIPS - k) % CHIPS) * 2 + 1 - core
        block = a_all.at[source]
        push(block, block, ss.at[k], sr.at[k], ctx=sibling).wait_recv()
    for k in range(1, DEPTH):
        block = b_all.at[(depth + DEPTH - k) % DEPTH]
        push(block, block, zs.at[k - 1], zr.at[k - 1], fsdp=depth).wait_recv()
    for copy in sends:
        copy.wait_send()
    for copy in own:
        copy.wait()


def gather_all(rows, weights):
    dma = pltpu.SemaphoreType.DMA
    return pl.pallas_call(
        gather_kernel,
        out_shape=(
            jax.ShapeDtypeStruct((2 * CHIPS,) + rows.shape, rows.dtype),
            jax.ShapeDtypeStruct((DEPTH,) + weights.shape, weights.dtype),
        ),
        in_specs=[ANY_SPEC] * 2,
        out_specs=(ANY_SPEC, ANY_SPEC),
        scratch_shapes=[dma((2,)), dma((3,)), dma((3,)), dma((3,)), dma((3,)), dma((4,)), dma((4,))],
        compiler_params=pltpu.CompilerParams(collective_id=1, has_side_effects=True),
    )(rows, weights)


PIECES = 4


def reduce_kernel(
    y_ref, w_ref, s_ref, y_out, w_all, s_out,
    pair, held, far, deep, small_z, small_c,
    pair_s, pair_r, far_s, far_r, zs, zr, cs, cr, ss, sr, sz_s, sz_r, sc_s, sc_r,
):
    me = lax.axis_index("ctx")
    depth = lax.axis_index("fsdp")
    core = me % 2
    chip = me // 2
    sibling = me + 1 - 2 * core
    context = 2 * CHIPS
    greet([(me + k) % context for k in range(1, context)], me, depth)
    part_rows = w_ref.shape[1] // PIECES
    sends = []

    def go(copy):
        copy.start()
        sends.append(copy)

    def peer(k):
        return ((chip + k) % CHIPS) * 2 + core

    def origin(k):
        return ((chip + CHIPS - k) % CHIPS) * 2 + core

    for k in range(1, DEPTH):
        target = (depth + k) % DEPTH
        go(push(s_ref, small_z.at[depth], sz_s.at[k - 1], sz_r.at[k - 1], fsdp=target))
    for k in (1, 2, 3, 0):
        block = ((chip + k) % CHIPS) * 2 + 1 - core
        go(push(y_ref.at[block], pair.at[k], pair_s.at[k], pair_r.at[k], ctx=sibling))
    deep_sends = []

    def send_piece(piece):
        rows = pl.ds(piece * part_rows, part_rows)
        copies = [
            push(
                w_ref.at[(depth + k) % DEPTH, rows],
                deep.at[k - 1, rows],
                zs.at[piece, k - 1],
                zr.at[piece, k - 1],
                fsdp=(depth + k) % DEPTH,
            )
            for k in range(1, DEPTH)
        ]
        for copy in copies:
            copy.start()
        deep_sends.append(copies)

    send_piece(0)
    send_piece(1)
    for k in (1, 2, 3, 0):
        push(pair.at[k], pair.at[k], pair_s.at[k], pair_r.at[k], ctx=sibling).wait_recv()
        joint = y_ref[peer(k)].astype(jnp.float32) + pair[k].astype(jnp.float32)
        if k:
            held[k - 1] = joint.astype(jnp.bfloat16)
            go(push(held.at[k - 1], far.at[k - 1], far_s.at[k - 1], far_r.at[k - 1], ctx=peer(k)))
        else:
            y_out[...] = joint
    small_z[depth] = s_ref[...]
    for k in range(1, DEPTH):
        slot = small_z.at[(depth + DEPTH - k) % DEPTH]
        push(slot, slot, sz_s.at[k - 1], sz_r.at[k - 1], fsdp=depth).wait_recv()
    small_c[me] = (small_z[0] + small_z[1]) + (small_z[2] + small_z[3])
    for k in range(1, context):
        slot = small_c.at[me]
        go(push(slot, slot, sc_s.at[k - 1], sc_r.at[k - 1], ctx=(me + k) % context))

    def hand_on(piece):
        rows = pl.ds(piece * part_rows, part_rows)
        for k in range(1, CHIPS):
            block = w_all.at[origin(k), rows]
            push(block, block, cs.at[piece, k - 1], cr.at[piece, k - 1], ctx=sibling).wait_recv()
            go(push(block, block, ss.at[piece, k], sr.at[piece, k], ctx=sibling))

    for piece in range(PIECES):
        rows = pl.ds(piece * part_rows, part_rows)
        total = w_ref[depth, rows].astype(jnp.float32)
        for k in range(1, DEPTH):
            slot = deep.at[k - 1, rows]
            push(slot, slot, zs.at[piece, k - 1], zr.at[piece, k - 1], fsdp=depth).wait_recv()
            total = total + deep[k - 1, rows].astype(jnp.float32)
        if piece + 2 < PIECES:
            for copy in deep_sends[piece]:
                copy.wait_send()
            send_piece(piece + 2)
        w_all[me, rows] = total.astype(jnp.bfloat16)
        block = w_all.at[me, rows]
        for k in range(1, CHIPS):
            go(push(block, block, cs.at[piece, k - 1], cr.at[piece, k - 1], ctx=peer(k)))
        go(push(block, block, ss.at[piece, 0], sr.at[piece, 0], ctx=sibling))
        if piece:
            hand_on(piece - 1)
    for k in range(1, CHIPS):
        slot = far.at[k - 1]
        push(slot, slot, far_s.at[k - 1], far_r.at[k - 1], ctx=sibling).wait_recv()
        y_out[...] += far[k - 1].astype(jnp.float32)
    for k in range(1, context):
        slot = small_c.at[(me + context - k) % context]
        push(slot, slot, sc_s.at[k - 1], sc_r.at[k - 1], ctx=sibling).wait_recv()
    total = small_c[0]
    for k in range(1, context):
        total = total + small_c[k]
    s_out[...] = total
    hand_on(PIECES - 1)
    for piece in range(PIECES):
        rows = pl.ds(piece * part_rows, part_rows)
        for k in range(CHIPS):
            block = w_all.at[((chip + CHIPS - k) % CHIPS) * 2 + 1 - core, rows]
            push(block, block, ss.at[piece, k], sr.at[piece, k], ctx=sibling).wait_recv()
    for copy in sends + deep_sends[PIECES - 2] + deep_sends[PIECES - 1]:
        copy.wait_send()


def reduce_all(partial, weight_grads, small):
    context, rows, columns = partial.shape
    dma = pltpu.SemaphoreType.DMA
    return pl.pallas_call(
        reduce_kernel,
        out_shape=(
            jax.ShapeDtypeStruct((rows, columns), jnp.float32),
            jax.ShapeDtypeStruct((context,) + weight_grads.shape[1:], jnp.bfloat16),
            jax.ShapeDtypeStruct(small.shape, jnp.float32),
        ),
        in_specs=[VMEM_SPEC] * 3,
        out_specs=(VMEM_SPEC,) * 3,
        scratch_shapes=[
            pltpu.VMEM((CHIPS, rows, columns), jnp.bfloat16),
            pltpu.VMEM((CHIPS - 1, rows, columns), jnp.bfloat16),
            pltpu.VMEM((CHIPS - 1, rows, columns), jnp.bfloat16),
            pltpu.VMEM((DEPTH - 1,) + weight_grads.shape[1:], jnp.bfloat16),
            pltpu.VMEM((DEPTH,) + small.shape, jnp.float32),
            pltpu.VMEM((context,) + small.shape, jnp.float32),
        ]
        + [dma((4,)), dma((4,)), dma((3,)), dma((3,))]
        + [dma((PIECES, 3))] * 4
        + [dma((PIECES, 4))] * 2
        + [dma((3,)), dma((3,)), dma((7,)), dma((7,))],
        compiler_params=pltpu.CompilerParams(
            collective_id=2, has_side_effects=True, vmem_limit_bytes=40 * 1024 * 1024
        ),
    )(partial, weight_grads, small)


Q_TILE = 256
PAIR = 2 * HEAD


def attention_kernel(
    joined_ref, dmix_ref, cos_ref, down_ref, up_ref, q_pl, q_low, k_pl,
    mix_ref, grad_ref, bias_ref, q_s, k_s, v_s, g_s, dk_s, dv_s,
):
    length = joined_ref.shape[0]
    scale = HEAD ** (-0.5)
    half = ROT // 2
    dot = lambda a, b, dims: lax.dot_general(a, b, dims, preferred_element_type=jnp.float32)
    contract_inner = (((1,), (0,)), ((), ()))

    def turn(block, sign):
        return (
            block * cos_ref[...]
            + pltpu.roll(block, PAIR - half, 1) * (sign * down_ref[...])
            + pltpu.roll(block, half, 1) * (sign * up_ref[...])
        )

    query = turn(joined_ref[:, :PAIR], 1.0)
    key = turn(joined_ref[:, PAIR : 2 * PAIR], 1.0)
    value = joined_ref[:, 2 * PAIR :]
    mix_grad = dmix_ref[...].astype(jnp.float32)
    lane = lax.broadcasted_iota(jnp.int32, (1, PAIR), 1)
    for head in range(2):
        own = (lane // HEAD) == head
        q_s[head] = jnp.where(own, query, 0.0).astype(jnp.bfloat16)
        k_s[head] = jnp.where(own, key, 0.0).astype(jnp.bfloat16)
        v_s[head] = jnp.where(own, value, 0.0).astype(jnp.bfloat16)
        g_s[head] = jnp.where(own, mix_grad, 0.0).astype(jnp.bfloat16)
    dk_s[...] = jnp.zeros_like(dk_s)
    dv_s[...] = jnp.zeros_like(dv_s)
    key_place = k_pl[...]
    dq_parts = []
    for tile in range(length // Q_TILE):
        rows = slice(tile * Q_TILE, (tile + 1) * Q_TILE)
        valid = (key_place <= q_pl[rows, :]) & (key_place >= q_low[rows, :])
        mixed = jnp.zeros((Q_TILE, PAIR), jnp.float32)
        d_query = jnp.zeros((Q_TILE, PAIR), jnp.float32)
        for head in range(2):
            q_t = q_s[head, rows, :]
            g_t = g_s[head, rows, :]
            score = jnp.where(valid, dot(q_t, k_s[head], contract_cols) * scale, masked_score)
            top = jnp.max(score, -1, keepdims=True)
            weight = jnp.exp(score - top)
            prob = weight * (1.0 / jnp.sum(weight, -1, keepdims=True))
            prob_low = prob.astype(jnp.bfloat16)
            mix_h = dot(prob_low, v_s[head], contract_inner)
            delta = jnp.sum(g_t.astype(jnp.float32) * mix_h, -1, keepdims=True)
            d_prob = dot(g_t, v_s[head], contract_cols)
            d_score = (prob * (d_prob - delta)).astype(jnp.bfloat16)
            d_query += dot(d_score, k_s[head], contract_inner)
            dk_s[...] += dot(d_score, q_t, contract_rows)
            dv_s[...] += dot(prob_low, g_t, contract_rows)
            mixed += mix_h
        mix_ref[rows, :] = mixed.astype(jnp.bfloat16)
        dq_parts.append(d_query)
    d_q = turn(jnp.concatenate(dq_parts, 0) * scale, -1.0)
    d_k = turn(dk_s[...] * scale, -1.0)
    for index, block in enumerate((d_q, d_k, dv_s[...])):
        columns = slice(index * PAIR, (index + 1) * PAIR)
        grad_ref[:, columns] = block.astype(jnp.bfloat16)
        bias_ref[:, columns] = jnp.sum(block, 0, keepdims=True)


def attention(joined, d_mix, tables, places, lowest):
    length = joined.shape[0]
    keep = [pltpu.VMEM((2, length, PAIR), jnp.bfloat16)] * 4
    return pl.pallas_call(
        attention_kernel,
        out_shape=(
            jax.ShapeDtypeStruct((length, PAIR), jnp.bfloat16),
            jax.ShapeDtypeStruct((length, 3 * PAIR), jnp.bfloat16),
            jax.ShapeDtypeStruct((1, 3 * PAIR), jnp.float32),
        ),
        in_specs=[VMEM_SPEC] * 8,
        out_specs=(VMEM_SPEC,) * 3,
        scratch_shapes=keep + [pltpu.VMEM((length, PAIR), jnp.float32)] * 2,
        compiler_params=pltpu.CompilerParams(vmem_limit_bytes=48 * 1024 * 1024),
    )(joined, d_mix, *tables, places[:, None], lowest[:, None], places[None, :])


def spread_kernel(holders, units, grads_ref, fused_ref, up_ref, down_ref, attn_ref):
    context, shard, _ = grads_ref.shape
    width = holders * PAIR
    ends = (3 * PAIR, 3 * PAIR + units, 3 * PAIR + 2 * units)
    for owner in range(context):
        own = slice(owner * units, (owner + 1) * units)
        up_ref[:, own] = grads_ref[owner, :, ends[0] : ends[1]].astype(jnp.float32)
        down_ref[:, own] = grads_ref[owner, :, ends[1] : ends[2]].astype(jnp.float32)
        if owner < holders:
            heads = slice(owner * PAIR, (owner + 1) * PAIR)
            attn_ref[:, heads] = grads_ref[owner, :, ends[2] :].astype(jnp.float32)
            for part in range(3):
                target = slice(part * width + owner * PAIR, part * width + (owner + 1) * PAIR)
                fused_ref[:, target] = grads_ref[
                    owner, :, part * PAIR : (part + 1) * PAIR
                ].astype(jnp.float32)


def spread_grads(grads, holders, units):
    context, shard, _ = grads.shape
    width = holders * PAIR
    shapes = ((shard, 3 * width), (shard, context * units), (shard, context * units), (shard, width))
    return pl.pallas_call(
        lambda *refs: spread_kernel(holders, units, *refs),
        out_shape=tuple(jax.ShapeDtypeStruct(shape, jnp.float32) for shape in shapes),
        in_specs=[VMEM_SPEC],
        out_specs=(VMEM_SPEC,) * 4,
        compiler_params=pltpu.CompilerParams(vmem_limit_bytes=32 * 1024 * 1024),
    )(grads)


def split_local(
    layer_input,
    cotangent,
    block_order,
    boundary,
    attn_gain,
    attn_shift,
    mlp_gain,
    mlp_shift,
    joined_weight,
    joined_bias,
    attn_weight,
    attn_bias,
    up_weight,
    up_bias,
    down_weight,
    down_bias,
):
    rows = layer_input.shape[1]
    width = layer_input.shape[2]
    context = 2 * CHIPS
    length = rows * context
    half = rows // 2
    holders = HEADS // 2
    shard = joined_weight.shape[0]
    units = up_weight.shape[1] // context
    me = lax.axis_index("ctx")
    slot = jnp.minimum(me, holders - 1)
    holds = me < holders

    own_joined = jnp.concatenate(
        [
            lax.dynamic_slice(joined_weight, (0, part * width + slot * PAIR), (shard, PAIR))
            for part in range(3)
        ],
        1,
    )
    own_attn = lax.dynamic_slice(attn_weight, (slot * PAIR, 0), (PAIR, shard)).T
    own_up = lax.dynamic_slice(up_weight, (0, me * units), (shard, units))
    own_down = lax.dynamic_slice(down_weight, (me * units, 0), (units, shard)).T
    own_weights = jnp.concatenate(
        [jnp.where(holds, own_joined, 0), jnp.where(holds, own_attn, 0)], 1
    )
    own_mlp = jnp.concatenate([own_up, own_down], 1)
    mlp_all = lax.all_gather(own_mlp, "fsdp", axis=0, tiled=True)
    own_rows = jnp.concatenate([layer_input[0], cotangent[0]], 1)
    rows_all, weights_all = gather_all(own_rows, own_weights)
    rows_all = rows_all.reshape(length, 2 * width)
    weights_all = weights_all.reshape(width, -1)
    w_joined = weights_all[:, : 3 * PAIR]
    w_attn = weights_all[:, 3 * PAIR :]
    hidden = rows_all[:, :width].astype(jnp.float32)
    grad_out = rows_all[:, width:]
    b_joined = jnp.where(
        holds,
        lax.dynamic_slice(joined_bias.reshape(3, width), (0, slot * PAIR), (3, PAIR)),
        0.0,
    ).reshape(3 * PAIR)
    b_up = lax.dynamic_slice(up_bias, (me * units,), (units,))

    places = place_lookup(block_order, jnp.int32(0), length, half)
    lowest = jnp.where(places >= boundary[0], boundary[0], 0)
    lane = jnp.arange(PAIR, dtype=jnp.int32) % HEAD
    bend = ROT // 2
    freq = 10000.0 ** (-2.0 * (lane % bend).astype(jnp.float32) / ROT)
    angles = places.astype(jnp.float32)[:, None] * freq[None, :]
    cosine = jnp.where(lane < ROT, jnp.cos(angles), 1.0)
    sine = jnp.sin(angles)
    tables = (
        cosine,
        jnp.where(lane < bend, -sine, 0.0),
        jnp.where((lane >= bend) & (lane < ROT), sine, 0.0),
    )

    normal, _ = normalize_parts(hidden)
    norm_attn = (normal * attn_gain + attn_shift).astype(jnp.bfloat16)
    norm_mlp = (normal * mlp_gain + mlp_shift).astype(jnp.bfloat16)
    joined = jnp.dot(norm_attn, w_joined, preferred_element_type=jnp.float32) + b_joined
    d_mix = jnp.dot(grad_out, w_attn, preferred_element_type=jnp.float32).astype(jnp.bfloat16)
    mix_low, d_joined_low, joined_sums = attention(joined, d_mix, tables, places, lowest)
    mlp_all, mix_low = lax.optimization_barrier((mlp_all, mix_low))
    w_up = mlp_all[:, :units]
    w_down = mlp_all[:, units:]
    upper = jnp.dot(norm_mlp, w_up, preferred_element_type=jnp.float32) + b_up
    d_act = jnp.dot(grad_out, w_down, preferred_element_type=jnp.float32)
    act, gelu_pull = jax.vjp(lambda argument: jax.nn.gelu(argument, approximate=False), upper)
    d_up = gelu_pull(d_act)[0]
    d_up_low = d_up.astype(jnp.bfloat16)
    outer = jnp.concatenate([act.astype(jnp.bfloat16), mix_low], 1)
    w_out = jnp.concatenate([w_down, w_attn], 1)
    branches = lax.dot_general(outer, w_out, contract_cols, preferred_element_type=jnp.float32)
    d_norm_attn = lax.dot_general(
        d_joined_low, w_joined, contract_cols, preferred_element_type=jnp.float32
    )
    d_norm_mlp = lax.dot_general(d_up_low, w_up, contract_cols, preferred_element_type=jnp.float32)
    scaled = d_norm_attn * attn_gain + d_norm_mlp * mlp_gain
    partial = jnp.concatenate([branches, scaled], 1).astype(jnp.bfloat16)
    weight_grads = jnp.concatenate(
        [
            lax.dot_general(norm_attn, d_joined_low, contract_rows, preferred_element_type=jnp.float32),
            lax.dot_general(norm_mlp, d_up_low, contract_rows, preferred_element_type=jnp.float32),
            lax.dot_general(grad_out, outer, contract_rows, preferred_element_type=jnp.float32),
        ],
        1,
    ).astype(jnp.bfloat16)
    mine = jnp.arange(context, dtype=jnp.int32) == me
    spread_joined = jnp.where(
        mine[:holders][None, :, None], joined_sums.reshape(3, 1, PAIR), 0.0
    ).reshape(-1)
    spread_up = jnp.where(mine[:, None], jnp.sum(d_up, 0)[None, :], 0.0).reshape(-1)
    small = jnp.concatenate(
        [
            jnp.sum(d_norm_attn * normal, 0),
            jnp.sum(d_norm_attn, 0),
            jnp.sum(d_norm_mlp * normal, 0),
            jnp.sum(d_norm_mlp, 0),
            spread_joined,
            jnp.sum(cotangent[0].astype(jnp.float32), 0),
            spread_up,
        ]
    )
    sums, grads, small = reduce_all(
        partial.reshape(context, rows, 2 * width),
        weight_grads.reshape(DEPTH, shard, -1),
        small.reshape(-1, 128),
    )
    small = small.reshape(-1)
    own_hidden = layer_input[0].astype(jnp.float32)
    layer_output = (own_hidden + sums[:, :width] + attn_bias + down_bias).astype(jnp.bfloat16)
    own_normal, own_inverse = normalize_parts(own_hidden)
    inner = sums[:, width:]
    back = own_inverse * (
        inner
        - jnp.mean(inner, -1, keepdims=True)
        - own_normal * jnp.mean(inner * own_normal, -1, keepdims=True)
    )
    input_grad = cotangent[0].astype(jnp.float32) + back
    dfused, dup, ddown, dattn = spread_grads(grads, holders, units)
    base = 4 * width
    fused_end = base + 3 * width
    out_end = fused_end + width
    return (
        layer_output[None],
        input_grad[None],
        small[:width],
        small[width : 2 * width],
        small[2 * width : 3 * width],
        small[3 * width : base],
        dfused,
        small[base:fused_end],
        dattn.T,
        small[fused_end:out_end],
        dup,
        small[out_end:],
        ddown.T,
        small[fused_end:out_end],
    )


def solution(mesh):
    split = mesh.shape["ctx"] == 2 * CHIPS and mesh.shape["fsdp"] == DEPTH
    return jax.shard_map(
        split_local if split else local,
        mesh=mesh,
        in_specs=(
            P("fsdp", "ctx", None),
            P("fsdp", "ctx", None),
            P(),
            P("fsdp"),
            P(),
            P(),
            P(),
            P(),
            P("fsdp", None),
            P(),
            P(None, "fsdp"),
            P(),
            P("fsdp", None),
            P(),
            P(None, "fsdp"),
            P(),
        ),
        out_specs=(
            P("fsdp", "ctx", None),
            P("fsdp", "ctx", None),
            P(),
            P(),
            P(),
            P(),
            P("fsdp", None),
            P(),
            P(None, "fsdp"),
            P(),
            P("fsdp", None),
            P(),
            P(None, "fsdp"),
            P(),
        ),
        check_vma=False,
    )
```
